32 devices in a mesh: energy: 8 (over z, x), slab: 4 (over y, core).
Axes of the slice: x: 2, y: 2, z: 4, core: 2. Of those that a mesh axis runs over, the one named last changes fastest.
Arguments:
- green: float32 [64, 4, 2, 256, 256], P(('energy', 'slab')), may hold values from -6 to 6
- phonon: float32 [32, 4, 2, 128, 128], P('energy', 'slab'), may hold values from -6 to 6
- coupling: float32 [256, 128], replicated, may hold values from -0.5 to 0.5
- occupation: float32 [32], replicated, may hold values from 0.1 to 3
- shifts: int32 [32], replicated, may hold values from 1 to 8, as said below
Outputs:
- sigma: float32 [64, 4, 2, 256, 256], P(('energy', 'slab'))
- polar: float32 [32, 4, 2, 128, 128], P('energy', 'slab')
The draws below stay inside these ranges and needn't reach their ends.
Inputs may be any that keep to these rules, and one draw needn't show every extreme that they name: `shifts`: some frequency has a shift of exactly 8.
All inputs are finite; a program needn't handle non-finite values.
Results may differ from the reference program's by a relative error of at most 0.0003.
Values sent between devices are 32-bit elements; how exact they have to be, the bound alone decides.
A program may use at most 192 MiB of HBM per device.

```python
import math
import jax
import jax.numpy as jnp
from jax import lax

B = 256
M = 128
E_OWN = 8
NE = 64
NW = 32
SLABS = 4


def draw_shifts(key, part):
    values = jax.random.randint(key, (NW,), 1, E_OWN + 1, dtype=jnp.int32)
    where = jax.random.randint(jax.random.fold_in(key, 7), (), 0, NW, dtype=jnp.int32)
    return values.at[where].set(E_OWN)


def level_of(rng, shape, split, low, top_value):
    def one(dim, blocks):
        draws = jax.random.uniform(jax.random.fold_in(jax.random.fold_in(rng, 6), dim), (blocks,), jnp.float32, low / len(split), top_value / len(split))
        return jnp.repeat(jnp.exp(draws), shape[dim] // blocks).reshape((-1,) + (1,) * (len(shape) - dim - 1))

    gain = one(*split[0])
    for cut in split[1:]:
        gain = gain * one(*cut)
    return gain


def normal_values(own_key, dims, scale, reach, pieces=(), kind=jnp.bfloat16):
    array = scale * jax.random.normal(own_key, dims, jnp.float32)
    if pieces:
        array = array * level_of(own_key, dims, pieces, -0.22, 0.18)
    return jnp.clip(array, -reach, reach).astype(kind)


def setup_inputs(seed: int = 0) -> dict:
    splits = jax.random.split(jax.random.key(seed), 6)
    green = normal_values(splits[0], (NE, SLABS, 2, B, B), 1.0, 6.0, ((0, 32),), jnp.float32)
    phonon = normal_values(splits[1], (NW, SLABS, 2, M, M), 1.0, 6.0, ((0, 8), (1, 4)), jnp.float32)
    coupling = normal_values(splits[2], (B, M), M ** -0.5, 0.5, (), jnp.float32)
    occupation = jnp.clip(jnp.exp(jax.random.uniform(splits[3], (NW,), jnp.float32, math.log(0.1), math.log(3.0))), 0.1, 3.0)
    shifts = draw_shifts(jax.random.fold_in(splits[5], 71), 0)
    return dict(green=green, phonon=phonon, coupling=coupling, occupation=occupation, shifts=shifts)


def lift_blocks(coupling, blocks):
    return jnp.einsum('im,...mk,jk->...ij', coupling, blocks, coupling, precision=lax.Precision.HIGHEST)

def lower_blocks(coupling, blocks):
    return jnp.einsum('bi,...bc,cj->...ij', coupling, blocks, coupling, precision=lax.Precision.HIGHEST)

def reference(green, phonon, coupling, occupation, shifts):
    total_e = green.shape[0]
    total_w = phonon.shape[0]
    margin = E_OWN
    zeros = jnp.zeros((margin,) + green.shape[1:], jnp.float32)
    padded = jnp.concatenate([zeros, green, zeros], axis=0)
    coupled = lift_blocks(coupling, phonon)
    emit = (occupation + 1.0)[:, None, None, None, None]
    absorb = occupation[:, None, None, None, None]
    sig_scale = 1.0 / math.sqrt(total_w)
    pol_scale = 1.0 / math.sqrt(total_e)

    def one_energy(index):
        above = jnp.take(padded, margin + index + shifts, axis=0)
        below = jnp.take(padded, margin + index - shifts, axis=0)
        mixed = emit * above + absorb * below
        real = lax.optimization_barrier(jnp.sum(coupled[:, :, 0] * mixed[:, :, 0] - coupled[:, :, 1] * mixed[:, :, 1], axis=0))
        imag = lax.optimization_barrier(jnp.sum(coupled[:, :, 0] * mixed[:, :, 1] + coupled[:, :, 1] * mixed[:, :, 0], axis=0))
        return jnp.stack([real, imag], axis=1) * sig_scale
    sigma = lax.map(one_energy, jnp.arange(total_e, dtype=jnp.int32))

    def one_shift(shift):
        part = lax.dynamic_slice_in_dim(padded, (margin + shift).astype(jnp.int32), total_e, 0)
        real = lax.optimization_barrier(jnp.sum(part[:, :, 0] * green[:, :, 0] + part[:, :, 1] * green[:, :, 1], axis=0))
        imag = lax.optimization_barrier(jnp.sum(part[:, :, 1] * green[:, :, 0] - part[:, :, 0] * green[:, :, 1], axis=0))
        return jnp.stack([real, imag], axis=1) * pol_scale
    pairs = lax.map(one_shift, shifts)
    polar = lower_blocks(coupling, pairs)
    return (sigma, polar)
```

```python
import functools
import math

import jax
import jax.numpy as jnp
from jax import lax
from jax.experimental import pallas as pl
from jax.experimental.pallas import tpu as pltpu
from jax.sharding import PartitionSpec as P

TILE = 8
LANES = 128
BLOCK = 4


def cell_of(low_ref, own_ref, high_ref):
    margin, count = low_ref.shape[0] if low_ref is not None else 0, own_ref.shape[0]

    def get(e, part, columns):
        if e < 0:
            return low_ref[e + margin, part, :, columns]
        if e >= count:
            return high_ref[e - count, part, :, columns]
        return own_ref[e, part, :, columns]

    return get


def sigma_kernel(low_ref, own_ref, high_ref, table_ref, out_ref):
    count, levels, width = own_ref.shape[0], high_ref.shape[0], own_ref.shape[3]
    get = cell_of(low_ref, own_ref, high_ref)
    for start in range(0, width, LANES):
        columns = slice(start, start + LANES)
        for first in range(0, count, BLOCK):
            block = range(first, min(first + BLOCK, count))
            real, imag = {}, {}
            for level in range(levels):
                for kind, step in ((0, level + 1), (1, -level - 1)):
                    c_re = table_ref[kind * levels + level, 0, :, columns]
                    c_im = table_ref[kind * levels + level, 1, :, columns]
                    for e in block:
                        g_re, g_im = get(e + step, 0, columns), get(e + step, 1, columns)
                        re = c_re * g_re - c_im * g_im
                        im = c_re * g_im + c_im * g_re
                        real[e] = real[e] + re if e in real else re
                        imag[e] = imag[e] + im if e in imag else im
            for e in block:
                out_ref[e, 0, :, columns] = real[e]
                out_ref[e, 1, :, columns] = imag[e]


def pairs_kernel(scale, own_ref, high_ref, out_ref):
    count, levels, width = own_ref.shape[0], high_ref.shape[0], own_ref.shape[3]
    get = cell_of(None, own_ref, high_ref)
    for start in range(0, width, LANES):
        columns = slice(start, start + LANES)
        for first in range(0, levels, BLOCK):
            block = range(first, min(first + BLOCK, levels))
            real, imag = {}, {}
            for e in range(count):
                o_re, o_im = get(e, 0, columns), get(e, 1, columns)
                for level in block:
                    p_re, p_im = get(e + level + 1, 0, columns), get(e + level + 1, 1, columns)
                    re = p_re * o_re + p_im * o_im
                    im = p_im * o_re - p_re * o_im
                    real[level] = real[level] + re if level in real else re
                    imag[level] = imag[level] + im if level in imag else im
            for level in block:
                out_ref[level, 0, :, columns] = real[level] * scale
                out_ref[level, 1, :, columns] = imag[level] * scale


def tiled(body, outer, *arrays):
    rows, width = arrays[0].shape[2:]

    def spec(n):
        return pl.BlockSpec((n, 2, TILE, width), lambda r: (0, 0, r, 0))

    moved = sum(a.size for a in arrays) + outer * 2 * rows * width
    return pl.pallas_call(
        body,
        grid=(rows // TILE,),
        in_specs=[spec(a.shape[0]) for a in arrays],
        out_specs=spec(outer),
        out_shape=jax.ShapeDtypeStruct((outer, 2, rows, width), jnp.float32),
        compiler_params=pltpu.CompilerParams(vmem_limit_bytes=32 * 1024 * 1024),
        cost_estimate=pl.CostEstimate(flops=16 * moved, bytes_accessed=4 * moved, transcendentals=0),
    )(*arrays)


def shards(green, phonon, coupling, occupation, shifts):
    n_energy, n_slab = lax.axis_size("energy"), lax.axis_size("slab")
    own, slabs, _, size, _ = green.shape
    halves = 2 if n_energy % 2 == 0 else 1
    team = halves * n_slab
    groups = [list(range(k, k + team)) for k in range(0, n_energy * n_slab, team)]
    both = ("energy", "slab")
    rows = size // halves
    levels = own * n_slab
    total_e = own * n_slab * n_energy

    every = lax.all_gather(phonon, "energy", axis=0, tiled=True)
    total_w = every.shape[0]

    pieces = green.reshape(own, slabs, 2, halves, rows, size).transpose(3, 1, 0, 2, 4, 5)
    pieces = pieces.reshape(team * own, 2, rows, size)
    mine = lax.all_to_all(pieces, both, 0, 0, axis_index_groups=groups, tiled=True)

    up = [(i, i + halves) for i in range(n_energy - halves)]
    down = [(i + halves, i) for i in range(n_energy - halves)]
    high = lax.ppermute(mine[:levels], "energy", down)
    low = lax.ppermute(mine[-levels:], "energy", up)

    share = lax.rem(lax.axis_index("energy"), halves) * rows
    my_coupling = lax.dynamic_slice_in_dim(coupling, share, rows, 0)

    steps = jnp.arange(1, levels + 1, dtype=jnp.int32)
    select = (shifts[None, :] == steps[:, None]).astype(jnp.float32) / math.sqrt(total_w)
    weights = jnp.concatenate([select * (occupation + 1.0)[None, :], select * occupation[None, :]], axis=0)
    mixed = jnp.dot(weights, every.reshape(total_w, -1), precision=lax.Precision.HIGHEST)
    mixed = mixed.reshape(2 * levels, 2, *every.shape[3:])
    half = jnp.einsum("im,lpmk->lpik", my_coupling, mixed, precision=lax.Precision.HIGH)
    tables = jnp.einsum("lpik,jk->lpij", half, coupling, precision=lax.Precision.HIGH)

    pairs = tiled(functools.partial(pairs_kernel, 1.0 / math.sqrt(total_e)), levels, mine, high)
    right = jnp.einsum("lpbc,cj->lpbj", pairs, coupling, precision=lax.Precision.HIGH)
    part = jnp.einsum("bi,lpbj->lpij", my_coupling, right, precision=lax.Precision.HIGH)
    total = lax.psum(part, "energy")
    own_w = phonon.shape[0]
    my_shifts = lax.dynamic_slice_in_dim(shifts, lax.axis_index("energy") * own_w, own_w, 0)
    chosen = (my_shifts[:, None] == steps[None, :])[:, :, None, None, None]
    polar = jnp.sum(jnp.where(chosen, total[None], 0.0), axis=1)[:, None]

    sigma_mine = tiled(sigma_kernel, team * own, low, mine, high, tables)
    back = lax.all_to_all(sigma_mine, both, 0, 0, axis_index_groups=groups, tiled=True)
    back = back.reshape(halves, slabs, own, 2, rows, size).transpose(2, 1, 3, 0, 4, 5)
    return (back.reshape(green.shape), polar)


def solution(mesh):
    placed = (
        P(("energy", "slab"), None, None, None, None),
        P("energy", "slab", None, None, None),
        P(),
        P(),
        P(),
    )
    return jax.shard_map(
        shards,
        mesh=mesh,
        in_specs=placed,
        out_specs=(
            P(("energy", "slab"), None, None, None, None),
            P("energy", "slab", None, None, None),
        ),
        check_vma=False,
    )
```

```python
import functools
import math

import jax
import jax.numpy as jnp
from jax import lax
from jax.experimental import pallas as pl
from jax.experimental.pallas import tpu as pltpu
from jax.sharding import PartitionSpec as P

TILE = 8
LANES = 128
BLOCK = 4


def cell_of(low_ref, own_ref, high_ref):
    margin, count = low_ref.shape[0] if low_ref is not None else 0, own_ref.shape[0]

    def get(e, part, columns):
        if e < 0:
            return low_ref[e + margin, part, :, columns]
        if e >= count:
            return high_ref[e - count, part, :, columns]
        return own_ref[e, part, :, columns]

    return get


def sigma_kernel(low_ref, own_ref, high_ref, table_ref, out_ref):
    count, levels, width = own_ref.shape[0], high_ref.shape[0], own_ref.shape[3]
    get = cell_of(low_ref, own_ref, high_ref)
    for start in range(0, width, LANES):
        columns = slice(start, start + LANES)
        for first in range(0, count, BLOCK):
            block = range(first, min(first + BLOCK, count))
            real, imag = {}, {}
            for level in range(levels):
                for kind, step in ((0, level + 1), (1, -level - 1)):
                    c_re = table_ref[kind * levels + level, 0, :, columns]
                    c_im = table_ref[kind * levels + level, 1, :, columns]
                    for e in block:
                        g_re, g_im = get(e + step, 0, columns), get(e + step, 1, columns)
                        re = c_re * g_re - c_im * g_im
                        im = c_re * g_im + c_im * g_re
                        real[e] = real[e] + re if e in real else re
                        imag[e] = imag[e] + im if e in imag else im
            for e in block:
                out_ref[e, 0, :, columns] = real[e]
                out_ref[e, 1, :, columns] = imag[e]


def pairs_kernel(scale, own_ref, high_ref, out_ref):
    count, levels, width = own_ref.shape[0], high_ref.shape[0], own_ref.shape[3]
    get = cell_of(None, own_ref, high_ref)
    for start in range(0, width, LANES):
        columns = slice(start, start + LANES)
        for first in range(0, levels, BLOCK):
            block = range(first, min(first + BLOCK, levels))
            real, imag = {}, {}
            for e in range(count):
                o_re, o_im = get(e, 0, columns), get(e, 1, columns)
                for level in block:
                    p_re, p_im = get(e + level + 1, 0, columns), get(e + level + 1, 1, columns)
                    re = p_re * o_re + p_im * o_im
                    im = p_im * o_re - p_re * o_im
                    real[level] = real[level] + re if level in real else re
                    imag[level] = imag[level] + im if level in imag else im
            for level in block:
                out_ref[level, 0, :, columns] = real[level] * scale
                out_ref[level, 1, :, columns] = imag[level] * scale


def tiled(body, outer, *arrays):
    rows, width = arrays[0].shape[2:]

    def spec(n):
        return pl.BlockSpec((n, 2, TILE, width), lambda r: (0, 0, r, 0))

    moved = sum(a.size for a in arrays) + outer * 2 * rows * width
    return pl.pallas_call(
        body,
        grid=(rows // TILE,),
        in_specs=[spec(a.shape[0]) for a in arrays],
        out_specs=spec(outer),
        out_shape=jax.ShapeDtypeStruct((outer, 2, rows, width), jnp.float32),
        compiler_params=pltpu.CompilerParams(vmem_limit_bytes=32 * 1024 * 1024),
        cost_estimate=pl.CostEstimate(flops=16 * moved, bytes_accessed=4 * moved, transcendentals=0),
    )(*arrays)


def shards(green, phonon, coupling, occupation, shifts):
    n_energy, n_slab = lax.axis_size("energy"), lax.axis_size("slab")
    own, slabs, _, size, _ = green.shape
    halves = 2 if n_energy % 2 == 0 else 1
    team = halves * n_slab
    groups = [list(range(k, k + team)) for k in range(0, n_energy * n_slab, team)]
    both = ("energy", "slab")
    rows = size // halves
    levels = own * n_slab
    total_e = own * n_slab * n_energy

    turns = n_energy // halves
    column = lax.rem(lax.axis_index("energy"), halves)
    lines = [[x + halves * z for z in range(turns)] for x in range(halves)]
    swap = [(i, i ^ 1) for i in range(n_energy)]
    every = lax.all_gather(phonon, "energy", axis=0, axis_index_groups=lines, tiled=True)
    own_w = phonon.shape[0]
    total_w = own_w * n_energy

    pieces = green.reshape(own, slabs, 2, halves, rows, size).transpose(3, 1, 0, 2, 4, 5)
    pieces = pieces.reshape(team * own, 2, rows, size)
    mine = lax.all_to_all(pieces, both, 0, 0, axis_index_groups=groups, tiled=True)

    up = [(i, i + halves) for i in range(n_energy - halves)]
    down = [(i + halves, i) for i in range(n_energy - halves)]

    my_coupling = lax.dynamic_slice_in_dim(coupling, column * rows, rows, 0)

    steps = jnp.arange(1, levels + 1, dtype=jnp.int32)
    select = (shifts[None, :] == steps[:, None]).astype(jnp.float32) / math.sqrt(total_w)
    weights = jnp.concatenate([select * (occupation + 1.0)[None, :], select * occupation[None, :]], axis=0)
    weights = weights.reshape(2 * levels, turns, halves, own_w)
    weights = lax.dynamic_index_in_dim(weights, column, 2, keepdims=False).reshape(2 * levels, -1)
    mixed = jnp.dot(weights, every.reshape(turns * own_w, -1), precision=lax.Precision.HIGHEST)
    mixed = mixed.reshape(2 * levels, 2, *every.shape[3:])
    mine, mixed = lax.optimization_barrier((mine, mixed))
    high = lax.ppermute(mine[:levels], "energy", down)
    low = lax.ppermute(mine[-levels:], "energy", up)
    if halves == 2:
        mixed = mixed + lax.ppermute(mixed, "energy", swap)
    half = jnp.einsum("im,lpmk->lpik", my_coupling, mixed, precision=lax.Precision.HIGH)
    tables = jnp.einsum("lpik,jk->lpij", half, coupling, precision=lax.Precision.HIGH)

    pairs = tiled(functools.partial(pairs_kernel, 1.0 / math.sqrt(total_e)), levels, mine, high)
    right = jnp.einsum("lpbc,cj->lpbj", pairs, coupling, precision=lax.Precision.HIGH)
    part = jnp.einsum("bi,lpbj->lpij", my_coupling, right, precision=lax.Precision.HIGH)
    low, part = lax.optimization_barrier((low, part))
    modes = part.shape[2] // halves
    kept = lax.dynamic_slice_in_dim(part, column * modes, modes, 2)
    if halves == 2:
        sent = lax.dynamic_slice_in_dim(part, (1 - column) * modes, modes, 2)
        kept = kept + lax.ppermute(sent, "energy", swap)
    sigma_mine = tiled(sigma_kernel, team * own, low, mine, high, tables)
    sigma_mine, kept = lax.optimization_barrier((sigma_mine, kept))
    total = lax.psum(kept, "energy", axis_index_groups=lines)

    def chosen(holder):
        own_shifts = lax.dynamic_slice_in_dim(shifts, holder * own_w, own_w, 0)
        taken = (own_shifts[:, None] == steps[None, :])[:, :, None, None, None]
        return jnp.sum(jnp.where(taken, total[None], 0.0), axis=1)

    polar = chosen(lax.axis_index("energy"))
    if halves == 2:
        other = lax.ppermute(chosen(lax.axis_index("energy") + 1 - 2 * column), "energy", swap)
        first, second = jnp.where(column == 0, polar, other), jnp.where(column == 0, other, polar)
        polar = jnp.concatenate([first, second], axis=2)
    polar = polar[:, None]

    back = lax.all_to_all(sigma_mine, both, 0, 0, axis_index_groups=groups, tiled=True)
    back = back.reshape(halves, slabs, own, 2, rows, size).transpose(2, 1, 3, 0, 4, 5)
    return (back.reshape(green.shape), polar)


def solution(mesh):
    placed = (
        P(("energy", "slab"), None, None, None, None),
        P("energy", "slab", None, None, None),
        P(),
        P(),
        P(),
    )
    return jax.shard_map(
        shards,
        mesh=mesh,
        in_specs=placed,
        out_specs=(
            P(("energy", "slab"), None, None, None, None),
            P("energy", "slab", None, None, None),
        ),
        check_vma=False,
    )
```

```python
import functools
import math

import jax
import jax.numpy as jnp
from jax import lax
from jax.experimental import pallas as pl
from jax.experimental.pallas import tpu as pltpu
from jax.sharding import PartitionSpec as P

TILE = 8
LANES = 128
BLOCK = 4
CHUNKS = 2


def cell_of(low_ref, own_ref, high_ref):
    margin, count = low_ref.shape[0] if low_ref is not None else 0, own_ref.shape[0]

    def get(e, part, columns):
        if e < 0:
            return low_ref[e + margin, part, :, columns]
        if e >= count:
            return high_ref[e - count, part, :, columns]
        return own_ref[e, part, :, columns]

    return get


def sigma_kernel(low_ref, own_ref, high_ref, table_ref, out_ref):
    count, levels, width = own_ref.shape[0], high_ref.shape[0], own_ref.shape[3]
    get = cell_of(low_ref, own_ref, high_ref)
    for start in range(0, width, LANES):
        columns = slice(start, start + LANES)
        for first in range(0, count, BLOCK):
            block = range(first, min(first + BLOCK, count))
            real, imag = {}, {}
            for level in range(levels):
                for kind, step in ((0, level + 1), (1, -level - 1)):
                    c_re = table_ref[kind * levels + level, 0, :, columns]
                    c_im = table_ref[kind * levels + level, 1, :, columns]
                    for e in block:
                        g_re, g_im = get(e + step, 0, columns), get(e + step, 1, columns)
                        re = c_re * g_re - c_im * g_im
                        im = c_re * g_im + c_im * g_re
                        real[e] = real[e] + re if e in real else re
                        imag[e] = imag[e] + im if e in imag else im
            for e in block:
                out_ref[e, 0, :, columns] = real[e]
                out_ref[e, 1, :, columns] = imag[e]


def pairs_kernel(scale, own_ref, high_ref, out_ref):
    count, levels, width = own_ref.shape[0], high_ref.shape[0], own_ref.shape[3]
    get = cell_of(None, own_ref, high_ref)
    for start in range(0, width, LANES):
        columns = slice(start, start + LANES)
        for first in range(0, levels, BLOCK):
            block = range(first, min(first + BLOCK, levels))
            real, imag = {}, {}
            for e in range(count):
                o_re, o_im = get(e, 0, columns), get(e, 1, columns)
                for level in block:
                    p_re, p_im = get(e + level + 1, 0, columns), get(e + level + 1, 1, columns)
                    re = p_re * o_re + p_im * o_im
                    im = p_im * o_re - p_re * o_im
                    real[level] = real[level] + re if level in real else re
                    imag[level] = imag[level] + im if level in imag else im
            for level in block:
                out_ref[level, 0, :, columns] = real[level] * scale
                out_ref[level, 1, :, columns] = imag[level] * scale


def tiled(body, outer, *arrays):
    rows, width = arrays[0].shape[2:]

    def spec(n):
        return pl.BlockSpec((n, 2, TILE, width), lambda r: (0, 0, r, 0))

    moved = sum(a.size for a in arrays) + outer * 2 * rows * width
    return pl.pallas_call(
        body,
        grid=(rows // TILE,),
        in_specs=[spec(a.shape[0]) for a in arrays],
        out_specs=spec(outer),
        out_shape=jax.ShapeDtypeStruct((outer, 2, rows, width), jnp.float32),
        compiler_params=pltpu.CompilerParams(vmem_limit_bytes=32 * 1024 * 1024),
        cost_estimate=pl.CostEstimate(flops=16 * moved, bytes_accessed=4 * moved, transcendentals=0),
    )(*arrays)


def shards(green, phonon, coupling, occupation, shifts):
    n_energy, n_slab = lax.axis_size("energy"), lax.axis_size("slab")
    own, slabs, _, size, _ = green.shape
    halves = 2 if n_energy % 2 == 0 else 1
    team = halves * n_slab
    groups = [list(range(k, k + team)) for k in range(0, n_energy * n_slab, team)]
    both = ("energy", "slab")
    rows = size // halves
    levels = own * n_slab
    total_e = own * n_slab * n_energy

    turns = n_energy // halves
    column = lax.rem(lax.axis_index("energy"), halves)
    lines = [[x + halves * z for z in range(turns)] for x in range(halves)]
    swap = [(i, i ^ 1) for i in range(n_energy)]
    every = lax.all_gather(phonon, "energy", axis=0, axis_index_groups=lines, tiled=True)
    own_w = phonon.shape[0]
    total_w = own_w * n_energy

    chunks = CHUNKS if rows % (CHUNKS * TILE) == 0 else 1
    depth = rows // chunks
    pieces = green.reshape(own, slabs, 2, halves, chunks, depth, size)
    up = [(i, i + halves) for i in range(n_energy - halves)]
    down = [(i + halves, i) for i in range(n_energy - halves)]
    mine, high, low = [], [], []
    for c in range(chunks):
        piece = pieces[:, :, :, :, c].transpose(3, 1, 0, 2, 4, 5).reshape(team * own, 2, depth, size)
        if c > 0:
            piece, mine[-1] = lax.optimization_barrier((piece, mine[-1]))
        mine.append(lax.all_to_all(piece, both, 0, 0, axis_index_groups=groups, tiled=True))
    mine[-1], every = lax.optimization_barrier((mine[-1], every))
    for c in range(chunks):
        high.append(lax.ppermute(mine[c][:levels], "energy", down))
        low.append(lax.ppermute(mine[c][-levels:], "energy", up))
    high[-1], low = lax.optimization_barrier((high[-1], low))
    my_coupling = [
        lax.dynamic_slice_in_dim(coupling, column * rows + c * depth, depth, 0) for c in range(chunks)
    ]

    steps = jnp.arange(1, levels + 1, dtype=jnp.int32)
    select = (shifts[None, :] == steps[:, None]).astype(jnp.float32) / math.sqrt(total_w)
    weights = jnp.concatenate([select * (occupation + 1.0)[None, :], select * occupation[None, :]], axis=0)
    weights = weights.reshape(2 * levels, turns, halves, own_w)
    weights = lax.dynamic_index_in_dim(weights, column, 2, keepdims=False).reshape(2 * levels, -1)
    mixed = jnp.dot(weights, every.reshape(turns * own_w, -1), precision=lax.Precision.HIGHEST)
    mixed = mixed.reshape(2 * levels, 2, *every.shape[3:])
    if halves == 2:
        mixed = mixed + lax.ppermute(mixed, "energy", swap)
    part = 0.0
    for c in range(chunks):
        pairs = tiled(functools.partial(pairs_kernel, 1.0 / math.sqrt(total_e)), levels, mine[c], high[c])
        right = jnp.einsum("lpbc,cj->lpbj", pairs, coupling, precision=lax.Precision.HIGH)
        part = part + jnp.einsum("bi,lpbj->lpij", my_coupling[c], right, precision=lax.Precision.HIGH)
    modes = part.shape[2] // halves
    kept = lax.dynamic_slice_in_dim(part, column * modes, modes, 2)
    if halves == 2:
        sent = lax.dynamic_slice_in_dim(part, (1 - column) * modes, modes, 2)
        kept = kept + lax.ppermute(sent, "energy", swap)
    back = []
    for c in range(chunks):
        half = jnp.einsum("im,lpmk->lpik", my_coupling[c], mixed, precision=lax.Precision.HIGH)
        table = jnp.einsum("lpik,jk->lpij", half, coupling, precision=lax.Precision.HIGH)
        sigma_mine = tiled(sigma_kernel, team * own, low[c], mine[c], high[c], table)
        if c == 0:
            sigma_mine, kept = lax.optimization_barrier((sigma_mine, kept))
        got = lax.all_to_all(sigma_mine, both, 0, 0, axis_index_groups=groups, tiled=True)
        back.append(got.reshape(halves, slabs, own, 2, depth, size))
    total = lax.psum(kept, "energy", axis_index_groups=lines)

    def chosen(holder):
        own_shifts = lax.dynamic_slice_in_dim(shifts, holder * own_w, own_w, 0)
        taken = (own_shifts[:, None] == steps[None, :])[:, :, None, None, None]
        return jnp.sum(jnp.where(taken, total[None], 0.0), axis=1)

    polar = chosen(lax.axis_index("energy"))
    if halves == 2:
        other = lax.ppermute(chosen(lax.axis_index("energy") + 1 - 2 * column), "energy", swap)
        first, second = jnp.where(column == 0, polar, other), jnp.where(column == 0, other, polar)
        polar = jnp.concatenate([first, second], axis=2)
    polar = polar[:, None]

    sigma = jnp.stack([g.transpose(2, 1, 3, 0, 4, 5) for g in back], axis=4)
    return (sigma.reshape(green.shape), polar)


def solution(mesh):
    placed = (
        P(("energy", "slab"), None, None, None, None),
        P("energy", "slab", None, None, None),
        P(),
        P(),
        P(),
    )
    return jax.shard_map(
        shards,
        mesh=mesh,
        in_specs=placed,
        out_specs=(
            P(("energy", "slab"), None, None, None, None),
            P("energy", "slab", None, None, None),
        ),
        check_vma=False,
    )
```

```python
import functools
import math

import jax
import jax.numpy as jnp
from jax import lax
from jax.experimental import pallas as pl
from jax.experimental.pallas import tpu as pltpu
from jax.sharding import PartitionSpec as P

TILE = 8
LANES = 128
BLOCK = 4
CHUNKS = 2


def cell_of(low_ref, own_ref, high_ref):
    margin, count = low_ref.shape[0] if low_ref is not None else 0, own_ref.shape[0]

    def get(e, part, columns):
        if e < 0:
            return low_ref[e + margin, part, :, columns]
        if e >= count:
            return high_ref[e - count, part, :, columns]
        return own_ref[e, part, :, columns]

    return get


def sigma_kernel(low_ref, own_ref, high_ref, table_ref, out_ref):
    count, levels, width = own_ref.shape[0], high_ref.shape[0], own_ref.shape[3]
    get = cell_of(low_ref, own_ref, high_ref)
    for start in range(0, width, LANES):
        columns = slice(start, start + LANES)
        for first in range(0, count, BLOCK):
            block = range(first, min(first + BLOCK, count))
            real, imag = {}, {}
            for level in range(levels):
                for kind, step in ((0, level + 1), (1, -level - 1)):
                    c_re = table_ref[kind * levels + level, 0, :, columns]
                    c_im = table_ref[kind * levels + level, 1, :, columns]
                    for e in block:
                        g_re, g_im = get(e + step, 0, columns), get(e + step, 1, columns)
                        re = c_re * g_re - c_im * g_im
                        im = c_re * g_im + c_im * g_re
                        real[e] = real[e] + re if e in real else re
                        imag[e] = imag[e] + im if e in imag else im
            for e in block:
                out_ref[e, 0, :, columns] = real[e]
                out_ref[e, 1, :, columns] = imag[e]


def pairs_kernel(scale, own_ref, high_ref, out_ref):
    count, levels, width = own_ref.shape[0], high_ref.shape[0], own_ref.shape[3]
    get = cell_of(None, own_ref, high_ref)
    for start in range(0, width, LANES):
        columns = slice(start, start + LANES)
        for first in range(0, levels, BLOCK):
            block = range(first, min(first + BLOCK, levels))
            real, imag = {}, {}
            for e in range(count):
                o_re, o_im = get(e, 0, columns), get(e, 1, columns)
                for level in block:
                    p_re, p_im = get(e + level + 1, 0, columns), get(e + level + 1, 1, columns)
                    re = p_re * o_re + p_im * o_im
                    im = p_im * o_re - p_re * o_im
                    real[level] = real[level] + re if level in real else re
                    imag[level] = imag[level] + im if level in imag else im
            for level in block:
                out_ref[level, 0, :, columns] = real[level] * scale
                out_ref[level, 1, :, columns] = imag[level] * scale


def tiled(body, outer, *arrays):
    rows, width = arrays[0].shape[2:]

    def spec(n):
        return pl.BlockSpec((n, 2, TILE, width), lambda r: (0, 0, r, 0))

    moved = sum(a.size for a in arrays) + outer * 2 * rows * width
    return pl.pallas_call(
        body,
        grid=(rows // TILE,),
        in_specs=[spec(a.shape[0]) for a in arrays],
        out_specs=spec(outer),
        out_shape=jax.ShapeDtypeStruct((outer, 2, rows, width), jnp.float32),
        compiler_params=pltpu.CompilerParams(vmem_limit_bytes=32 * 1024 * 1024),
        cost_estimate=pl.CostEstimate(flops=16 * moved, bytes_accessed=4 * moved, transcendentals=0),
    )(*arrays)


def shards(green, phonon, coupling, occupation, shifts):
    n_energy, n_slab = lax.axis_size("energy"), lax.axis_size("slab")
    own, slabs, _, size, _ = green.shape
    halves = 2 if n_energy % 2 == 0 else 1
    team = halves * n_slab
    groups = [list(range(k, k + team)) for k in range(0, n_energy * n_slab, team)]
    both = ("energy", "slab")
    rows = size // halves
    levels = own * n_slab
    total_e = own * n_slab * n_energy

    turns = n_energy // halves
    column = lax.rem(lax.axis_index("energy"), halves)
    lines = [[x + halves * z for z in range(turns)] for x in range(halves)]
    swap = [(i, i ^ 1) for i in range(n_energy)]
    every = lax.all_gather(phonon, "energy", axis=0, axis_index_groups=lines, tiled=True)
    own_w = phonon.shape[0]
    total_w = own_w * n_energy

    chunks = CHUNKS if rows % (CHUNKS * TILE) == 0 else 1
    depth = rows // chunks
    pieces = green.reshape(own, slabs, 2, halves, chunks, depth, size)
    up = [(i, i + halves) for i in range(n_energy - halves)]
    down = [(i + halves, i) for i in range(n_energy - halves)]
    mine, high, low = [], [], []
    for c in range(chunks):
        piece = pieces[:, :, :, :, c].transpose(3, 1, 0, 2, 4, 5).reshape(team * own, 2, depth, size)
        if c > 0:
            piece, mine[-1] = lax.optimization_barrier((piece, mine[-1]))
        mine.append(lax.all_to_all(piece, both, 0, 0, axis_index_groups=groups, tiled=True))
    mine[-1], every = lax.optimization_barrier((mine[-1], every))
    for c in range(chunks):
        high.append(lax.ppermute(mine[c][:levels], "energy", down))
        low.append(lax.ppermute(mine[c][-levels:], "energy", up))
    high[-1], low = lax.optimization_barrier((high[-1], low))
    my_coupling = [
        lax.dynamic_slice_in_dim(coupling, column * rows + c * depth, depth, 0) for c in range(chunks)
    ]

    steps = jnp.arange(1, levels + 1, dtype=jnp.int32)
    select = (shifts[None, :] == steps[:, None]).astype(jnp.float32) / math.sqrt(total_w)
    weights = jnp.concatenate([select * (occupation + 1.0)[None, :], select * occupation[None, :]], axis=0)
    weights = weights.reshape(2 * levels, turns, halves, own_w)
    weights = lax.dynamic_index_in_dim(weights, column, 2, keepdims=False).reshape(2 * levels, -1)
    mixed = jnp.dot(weights, every.reshape(turns * own_w, -1), precision=lax.Precision.HIGHEST)
    mixed = mixed.reshape(2 * levels, 2, *every.shape[3:])
    if halves == 2:
        mixed = mixed + lax.ppermute(mixed, "energy", swap)
    part = 0.0
    for c in range(chunks):
        pairs = tiled(functools.partial(pairs_kernel, 1.0 / math.sqrt(total_e)), levels, mine[c], high[c])
        right = jnp.einsum("lpbc,cj->lpbj", pairs, coupling, precision=lax.Precision.HIGH)
        part = part + jnp.einsum("bi,lpbj->lpij", my_coupling[c], right, precision=lax.Precision.HIGH)
    mixed, part = lax.optimization_barrier((mixed, part))
    total = lax.psum(part, "energy", axis_index_groups=lines)

    back = []
    for c in range(chunks):
        half = jnp.einsum("im,lpmk->lpik", my_coupling[c], mixed, precision=lax.Precision.HIGH)
        table = jnp.einsum("lpik,jk->lpij", half, coupling, precision=lax.Precision.HIGH)
        sigma_mine = tiled(sigma_kernel, team * own, low[c], mine[c], high[c], table)
        if c == 0:
            sigma_mine, total = lax.optimization_barrier((sigma_mine, total))
        got = lax.all_to_all(sigma_mine, both, 0, 0, axis_index_groups=groups, tiled=True)
        back.append(got.reshape(halves, slabs, own, 2, depth, size))

    def chosen(holder):
        own_shifts = lax.dynamic_slice_in_dim(shifts, holder * own_w, own_w, 0)
        taken = (own_shifts[:, None] == steps[None, :])[:, :, None, None, None]
        return jnp.sum(jnp.where(taken, total[None], 0.0), axis=1)

    polar = chosen(lax.axis_index("energy"))
    if halves == 2:
        polar = polar + lax.ppermute(chosen(lax.axis_index("energy") + 1 - 2 * column), "energy", swap)
    polar = polar[:, None]

    sigma = jnp.stack([g.transpose(2, 1, 3, 0, 4, 5) for g in back], axis=4)
    return (sigma.reshape(green.shape), polar)


def solution(mesh):
    placed = (
        P(("energy", "slab"), None, None, None, None),
        P("energy", "slab", None, None, None),
        P(),
        P(),
        P(),
    )
    return jax.shard_map(
        shards,
        mesh=mesh,
        in_specs=placed,
        out_specs=(
            P(("energy", "slab"), None, None, None, None),
            P("energy", "slab", None, None, None),
        ),
        check_vma=False,
    )
```
